32 devices in a mesh: inst: 8 (over y, x, core), tp: 4 (over z).
Axes of the slice: x: 2, y: 2, z: 4, core: 2. Of those that a mesh axis runs over, the one named last changes fastest.
Arguments:
- x_steps: bfloat16 [4, 8, 8, 8192], P(None, 'inst'), may hold values from -6 to 6
- w_query: bfloat16 [8192, 4096], P(None, 'tp'), may hold values from -0.0625 to 0.0625
- w_key: bfloat16 [8192, 1024], P(None, 'tp'), may hold values from -0.0625 to 0.0625
- w_value: bfloat16 [8192, 1024], P(None, 'tp'), may hold values from -0.0625 to 0.0625
- w_out: bfloat16 [4096, 8192], P('tp'), may hold values from -1.1953125 to 1.1953125
- k_pool: bfloat16 [8, 64, 64, 1024], P('inst', None, None, 'tp'), may hold values from -600 to 600
- v_pool: bfloat16 [8, 64, 64, 1024], P('inst', None, None, 'tp'), may hold values from -6 to 6
- page_table: int32 [8, 64], P('inst'), may hold values from 0 to 63, each once within a row
- lengths: int32 [8, 8], P('inst'), may hold values from 1 to 508, 2560 in all within a row
- source_instance: int32 [8, 8], replicated, may hold values from 0 to 7, as said below
- source_slot: int32 [8, 8], replicated, may hold values from 0 to 7, as said below
Outputs:
- layer_out: bfloat16 [4, 8, 8, 8192], P(None, 'inst', None, 'tp')
- key_cache: bfloat16 [8, 8, 512, 1024], P('inst', None, None, 'tp')
- value_cache: bfloat16 [8, 8, 512, 1024], P('inst', None, None, 'tp')
The draws below stay inside these ranges and needn't reach their ends.
Inputs may be any that keep to these rules, and one draw needn't show every extreme that they name: `page_table`: each instance's row is a permutation of its pages; request r owns entries r * 8 to r * 8 + 7 in order of position. Each instance's 8 lengths sum to 2560. source_instance and source_slot form a permutation of all slots; exactly 7 slots of each instance take a request from another instance, the rest keep their own (source is the slot itself); at most one request goes from one instance to another, and this is reached. `source_slot`: see source_instance.
All inputs are finite; a program needn't handle non-finite values.
Results may differ from the reference program's by a relative error of at most 0.0055.
The reference program's roundings to bfloat16 on the way count: a program that leaves them out, or rounds other values in their place, can miss the bound.
Values may be sent and summed in bfloat16 or wider, within the bound.
A program may use at most 192 MiB of HBM per device.

```python
import math
import jax
import jax.numpy as jnp
import numpy as np
from jax import lax

D = 8192
HD = 128
KVH = 8
HEADS = 32
REQ = 8
PAGE = 64
PMAX = 8
STEPS = 4
INST = 8
POOL = 64
LEN_MOST = 508
LEN_MEAN = 320
MOVE = 7
N_INST = 8


def plan_tables(key):
    keys = jax.random.split(key, 3)
    order = jax.random.permutation(keys[0], N_INST).astype(jnp.int32)
    rank = jnp.argsort(order, stable=True).astype(jnp.int32)
    offsets = (jax.random.permutation(keys[1], N_INST - 1)[:MOVE] + 1).astype(jnp.int32)
    slot_keys = jax.random.split(keys[2], N_INST)
    moving = jax.vmap(lambda single: jax.random.permutation(single, REQ)[:MOVE])(slot_keys).astype(jnp.int32)
    sources = order[(rank[:, None] - offsets[None, :]) % N_INST]
    source_slots = moving[sources, jnp.arange(MOVE, dtype=jnp.int32)[None, :]]
    rows = jnp.arange(N_INST, dtype=jnp.int32)[:, None]
    base_inst = jnp.broadcast_to(rows, (N_INST, REQ))
    base_slot = jnp.broadcast_to(jnp.arange(REQ, dtype=jnp.int32)[None, :], (N_INST, REQ))
    inst_table = base_inst.at[rows, moving].set(sources)
    slot_table = base_slot.at[rows, moving].set(source_slots)
    return (inst_table.astype(jnp.int32), slot_table.astype(jnp.int32))


def draw_source_instance(key, part):
    tables = plan_tables(key)
    return tables[0]


def draw_source_slot(key, part):
    tables = plan_tables(key)
    return tables[1]


def draw_k_pool(key, part):
    key = jax.random.fold_in(key, 11)
    shape = (N_INST, POOL, PAGE, KVH * HD)
    values = jax.random.truncated_normal(key, -6.0, 6.0, shape, jnp.float32)
    return values.astype(jnp.bfloat16)


def level_of(rng, shape, cuts, low, top_value):
    def one(axis_at, shards_of):
        heights = jax.random.uniform(jax.random.fold_in(jax.random.fold_in(rng, 6), axis_at), (shards_of,), jnp.float32, low / len(cuts), top_value / len(cuts))
        return jnp.repeat(jnp.exp(heights), shape[axis_at] // shards_of).reshape((-1,) + (1,) * (len(shape) - axis_at - 1))

    factor_of = one(*cuts[0])
    for cut in cuts[1:]:
        factor_of = factor_of * one(*cut)
    return factor_of


def profile(number_of, total, most, lean):
    weights = [(1 << 20) // math.isqrt(standing ** lean) + 1 for standing in range(2, number_of + 1)]
    spare, holding = total - most - (number_of - 1), [1] * (number_of - 1)
    while spare > 0:
        candidates = [i for i in range(number_of - 1) if holding[i] < most]
        mass, left = sum([weights[i] for i in candidates]), spare
        for i in candidates:
            more = min(most - holding[i], max(1, left * weights[i] // mass), spare)
            holding[i] = holding[i] + more
            spare = spare - more
    return np.array([most] + holding)


def uneven_parts(rng, amount, total, most, lean):
    if amount == 2:
        one = jax.random.randint(rng, (), max(1, total - most), min(most, total - 1) + 1)
        return jnp.stack([one, total - one])
    tallies = jnp.asarray(profile(amount, total, most, lean), jnp.int32)
    couples = (amount - 1) // 2
    source_of, taker = tallies[1:1 + 2 * couples:2], tallies[2:2 + 2 * couples:2]
    margin = jnp.minimum(source_of - 1, most - taker)
    shifted = jax.random.randint(jax.random.fold_in(rng, 1), (couples,), 0, 1 << 20) % (margin + 1)
    tallies = tallies.at[1:1 + 2 * couples:2].set(source_of - shifted).at[2:2 + 2 * couples:2].set(taker + shifted)
    return tallies[jax.random.permutation(jax.random.fold_in(rng, 2), amount)]


def noise(rng, dims, width, limit, cuts=(), kind=jnp.bfloat16):
    values = width * jax.random.normal(rng, dims, jnp.float32)
    if cuts:
        values = values * level_of(rng, dims, cuts, -0.22, 0.18)
    return jnp.clip(values, -limit, limit).astype(kind)


def setup_inputs(seed: int = 0) -> dict:
    seeds = jax.random.split(jax.random.key(seed), 12)
    x_steps = noise(seeds[0], (STEPS, INST, REQ, D), 1.0, 6.0, ((1, 8),))
    w_query = noise(seeds[1], (D, HEADS * HD), D ** -0.5, 0.0625, ((1, 4),))
    w_key = noise(seeds[2], (D, KVH * HD), D ** -0.5, 0.0625, ((1, 4),))
    w_value = noise(seeds[3], (D, KVH * HD), D ** -0.5, 0.0625, ((1, 4),))
    w_out = noise(seeds[4], (HEADS * HD, D), 0.2, 1.1953125, ((0, 4),))
    k_pool = draw_k_pool(jax.random.fold_in(seeds[11], 71), 0)
    v_pool = noise(seeds[6], (INST, POOL, PAGE, KVH * HD), 1.0, 6.0, ((0, 8), (3, 4)))
    page_table = jax.vmap(lambda own: jax.random.permutation(own, POOL))(jax.random.split(seeds[7], INST)).reshape((INST, POOL)).astype(jnp.int32)
    lengths = jax.vmap(lambda own: uneven_parts(own, REQ, REQ * LEN_MEAN, LEN_MOST, 2))(jax.random.split(seeds[8], INST)).reshape((INST, REQ)).astype(jnp.int32)
    source_instance = draw_source_instance(jax.random.fold_in(seeds[11], 71), 0)
    source_slot = draw_source_slot(jax.random.fold_in(seeds[11], 71), 0)
    return {"x_steps": x_steps, "w_query": w_query, "w_key": w_key, "w_value": w_value, "w_out": w_out, "k_pool": k_pool, "v_pool": v_pool, "page_table": page_table, "lengths": lengths, "source_instance": source_instance, "source_slot": source_slot}


rope_base = 500000.0

def rotary(vectors, positions):
    half = vectors.shape[-1] // 2
    freqs = rope_base ** (-(jnp.arange(half, dtype=jnp.float32) * 2.0 / vectors.shape[-1]))
    angles = positions.astype(jnp.float32)[..., None] * freqs
    cosine = jnp.cos(angles)
    sine = jnp.sin(angles)
    first = vectors[..., :half]
    second = vectors[..., half:]
    return jnp.concatenate([first * cosine - second * sine, second * cosine + first * sine], axis=-1)

def decode_step(key_view, value_view, lengths_now, tokens, w_query, w_key, w_value, w_out):
    query = jnp.dot(tokens, w_query, preferred_element_type=jnp.float32).reshape(REQ, KVH, HEADS // KVH, HD)
    fresh_key = jnp.dot(tokens, w_key, preferred_element_type=jnp.float32).reshape(REQ, KVH, HD)
    fresh_value = jnp.dot(tokens, w_value, preferred_element_type=jnp.float32).reshape(REQ, KVH, HD)
    query = rotary(query, lengths_now[:, None, None]).astype(jnp.bfloat16)
    fresh_key = rotary(fresh_key, lengths_now[:, None]).astype(jnp.bfloat16)
    fresh_value = fresh_value.astype(jnp.bfloat16)
    places = jnp.arange(PMAX * PAGE, dtype=jnp.int32)
    hit = (places[None, :] == lengths_now[:, None])[:, :, None, None]
    key_view = jnp.where(hit, fresh_key[:, None], key_view)
    value_view = jnp.where(hit, fresh_value[:, None], value_view)
    scores = jnp.einsum('rkgd,rckd->rkgc', query.astype(jnp.float32), key_view.astype(jnp.float32)) / math.sqrt(HD)
    valid = (places[None, :] <= lengths_now[:, None])[:, None, None, :]
    scores = jnp.where(valid, scores, -jnp.inf)
    top = lax.optimization_barrier(jnp.max(scores, axis=-1, keepdims=True))
    weights = jnp.exp(scores - top)
    weights = (weights / lax.optimization_barrier(jnp.sum(weights, axis=-1, keepdims=True))).astype(jnp.bfloat16)
    mixed = jnp.einsum('rkgc,rckd->rkgd', weights.astype(jnp.float32), value_view.astype(jnp.float32)).astype(jnp.bfloat16)
    output = jnp.dot(mixed.reshape(REQ, HEADS * HD), w_out, preferred_element_type=jnp.float32).astype(jnp.bfloat16)
    return (key_view, value_view, lengths_now + 1, output)

def run_phase(key_views, value_views, lengths_now, phase_x, w_query, w_key, w_value, w_out):

    def one_instance(packed):
        key_view, value_view, current, tokens_all = packed
        results = []
        for turn in range(tokens_all.shape[0]):
            key_view, value_view, current, output = decode_step(key_view, value_view, current, tokens_all[turn], w_query, w_key, w_value, w_out)
            results.append(output)
        return (key_view, value_view, current, jnp.stack(results))
    return lax.map(one_instance, (key_views, value_views, lengths_now, phase_x))

def reference(x_steps, w_query, w_key, w_value, w_out, k_pool, v_pool, page_table, lengths, source_instance, source_slot):
    table = page_table.reshape(N_INST, REQ, PMAX)

    def views_of(pair):
        return pair[0][pair[1]].reshape(REQ, PMAX * PAGE, KVH, HD)
    key_views = lax.map(views_of, (k_pool, table))
    value_views = lax.map(views_of, (v_pool, table))
    first_x = jnp.transpose(x_steps[:2], (1, 0, 2, 3))
    second_x = jnp.transpose(x_steps[2:], (1, 0, 2, 3))
    key_views, value_views, current, first_out = run_phase(key_views, value_views, lengths, first_x, w_query, w_key, w_value, w_out)
    key_views = key_views[source_instance, source_slot]
    value_views = value_views[source_instance, source_slot]
    current = current[source_instance, source_slot]
    key_views, value_views, current, second_out = run_phase(key_views, value_views, current, second_x, w_query, w_key, w_value, w_out)
    joined = jnp.concatenate([first_out, second_out], axis=1)
    layer_out = jnp.transpose(joined, (1, 0, 2, 3))
    key_cache = key_views.reshape(N_INST, REQ, PMAX * PAGE, KVH * HD)
    value_cache = value_views.reshape(N_INST, REQ, PMAX * PAGE, KVH * HD)
    return (layer_out, key_cache, value_cache)
```

```python
import functools
import math

import jax
import jax.numpy as jnp
from jax import lax
from jax.experimental import pallas as pl
from jax.experimental.pallas import tpu as pltpu
from jax.sharding import PartitionSpec as P

HD = 128
GROUP = 4
MESH = pl.DeviceIdType.MESH

rope_base = 500000.0
F32 = jnp.float32
BF16 = jnp.bfloat16


def angles_of(positions):
    half = HD // 2
    freqs = rope_base ** (-(jnp.arange(half, dtype=F32) * 2.0 / HD))
    angles = positions.astype(F32)[..., None] * freqs
    cosine = jnp.cos(angles)
    sine = jnp.sin(angles)
    return jnp.concatenate([cosine, cosine], -1), jnp.concatenate([-sine, sine], -1)


def rotate(vectors, cosine, sine):
    return vectors * cosine + pltpu.roll(vectors, HD // 2, 1) * sine


def rounded(value):
    return value.astype(BF16).astype(F32)


def fused(
    n, t, req, page, chunk, tile,
    tab, cos_ref, sin_ref, x_ref, wq, wk, wv, wo, kp, vp,
    layer, staged,
    pool, send, recv, ext, ext_in, view, wq_b, wk_b, wv_b, wo_b, acc,
    q_s, k_s, kr_s, v_s, m1, m2, mix, rs_out, rs_in,
    pool_sem, w_sem, wo_sem, kv_ss, kv_rs, ex_ss, ex_rs, rs_ss, rs_rs, out_sem,
):
    me = lax.axis_index("inst")
    tp = lax.axis_index("tp")
    feats = kp.shape[2]
    heads = wq.shape[1] // HD
    kvs = feats // HD
    pmax = kp.shape[0] // req
    depth = wq.shape[0]
    steps = depth // chunk
    bufs = wq_b.shape[0]
    width = layer.shape[1]
    at_own, at_slot, at_rel, at_len, at_page = 0, n, 2 * n, 2 * n + req, 2 * n + 2 * req

    pools = [pltpu.make_async_copy(src, pool.at[i], pool_sem.at[i]) for i, src in enumerate((kp, vp))]
    for c in pools:
        c.start()

    def weights(i):
        slot = lax.rem(i, bufs)
        rows = pl.ds(pl.multiple_of(i * chunk, chunk), chunk)
        return [
            pltpu.make_async_copy(src.at[rows], dst.at[slot], w_sem.at[j, slot])
            for j, (src, dst) in enumerate(((wq, wq_b), (wk, wk_b), (wv, wv_b)))
        ]

    barrier = pltpu.get_barrier_semaphore()

    @pl.loop(1, n)
    def _(k):
        pl.semaphore_signal(
            barrier, inc=1, device_id=(lax.rem(me + k, n), tp), device_id_type=MESH
        )

    @pl.loop(1, t)
    def _(k):
        pl.semaphore_signal(
            barrier, inc=1, device_id=(me, lax.rem(tp + k, t)), device_id_type=MESH
        )

    for c in pools:
        c.wait()
    for i in range(bufs - 1):
        for c in weights(i):
            c.start()
    pl.semaphore_wait(barrier, n - 1 + t - 1)

    def move(k):
        return pltpu.make_async_remote_copy(
            src_ref=send.at[k], dst_ref=recv.at[k], send_sem=kv_ss.at[k], recv_sem=kv_rs.at[k],
            device_id=(lax.rem(me + k, n), tp), device_id_type=MESH,
        )

    def move_ext(k):
        return pltpu.make_async_remote_copy(
            src_ref=ext.at[k], dst_ref=ext_in.at[k], send_sem=ex_ss.at[k], recv_sem=ex_rs.at[k],
            device_id=(lax.rem(me + k, n), tp), device_id_type=MESH,
        )

    @pl.loop(1, n)
    def _(k):
        slot = tab[at_own + k]
        for c in range(pmax):
            at = tab[at_page + slot * pmax + c]
            for i in range(2):
                send[k, i, c * page : (c + 1) * page, :] = pool[i, at]
        move(k).start()

    own = tab[at_own]
    for c in range(pmax):
        at = tab[at_page + own * pmax + c]
        for i in range(2):
            recv[0, i, c * page : (c + 1) * page, :] = pool[i, at]

    acc[...] = jnp.zeros_like(acc)
    qw = heads * HD

    @pl.loop(0, steps)
    def _(i):
        @pl.when(i + bufs - 1 < steps)
        def _():
            for c in weights(i + bufs - 1):
                c.start()

        for c in weights(i):
            c.wait()
        slot = lax.rem(i, bufs)
        xs = x_ref[:, pl.ds(pl.multiple_of(i * chunk, chunk), chunk)]
        acc[:, :qw] += jnp.dot(xs, wq_b[slot], preferred_element_type=F32)
        acc[:, qw : qw + feats] += jnp.dot(xs, wk_b[slot], preferred_element_type=F32)
        acc[:, qw + feats :] += jnp.dot(xs, wv_b[slot], preferred_element_type=F32)

    load_out = pltpu.make_async_copy(wo, wo_b, wo_sem)
    load_out.start()

    for turn in range(4):
        rows = slice(turn * req, (turn + 1) * req)
        for h in range(heads):
            q_s[(turn * heads + h) * req : (turn * heads + h + 1) * req, :] = acc[rows, h * HD : (h + 1) * HD]
        for h in range(kvs):
            part = acc[rows, qw + h * HD : qw + (h + 1) * HD]
            k_s[(turn * kvs + h) * req : (turn * kvs + h + 1) * req, :] = part
            if turn < 2:
                kr_s[rows, h * HD : (h + 1) * HD] = rounded(rotate(part, cos_ref[rows, :], sin_ref[rows, :]))
    v_s[...] = rounded(acc[:, qw + feats :])

    @pl.loop(0, n)
    def _(k):
        slot = tab[at_own + k]
        for turn in range(2):
            ext[k, turn : turn + 1, :] = kr_s[pl.ds(turn * req + slot, 1), :]
            ext[k, 2 + turn : 3 + turn, :] = v_s[pl.ds(turn * req + slot, 1), :]
            ext[k, 4 + turn : 5 + turn, :HD] = cos_ref[pl.ds((2 + turn) * req + slot, 1), :]
            ext[k, 6 + turn : 7 + turn, :HD] = sin_ref[pl.ds((2 + turn) * req + slot, 1), :]
        ext[k, 8:9, :] = jnp.full((1, feats), tab[at_len + slot], jnp.int32).astype(F32)
        ext[k, 9:16, :] = jnp.zeros((7, feats), F32)

        @pl.when(k > 0)
        def _():
            move_ext(k).start()

    ext_in[0] = ext[0]

    spots = lax.broadcasted_iota(jnp.int32, (page, feats), 0).astype(F32)

    def inserted(block, c, first, fresh):
        block = block.astype(F32)
        for i, row in enumerate(fresh):
            block = jnp.where(spots == first + (i - c * page), row, block)
        return block.astype(BF16)

    row_q = lax.broadcasted_iota(jnp.int32, (2 * heads, HD), 0)
    late_q = row_q >= heads
    kv_q = lax.rem(row_q, heads) // GROUP

    def attend(base, slot, cosines, sines, first, keys, values):
        q = q_s[pl.ds(base * heads * req + slot, 2 * heads, stride=req), :]
        cosine = jnp.where(late_q, cosines[1], cosines[0])
        sine = jnp.where(late_q, sines[1], sines[0])
        q = rotate(q, cosine, sine)
        q = jnp.concatenate([jnp.where(kv_q == h, q, 0.0) for h in range(kvs)], axis=1).astype(BF16)
        scores = lax.dot_general(q, keys, (((1,), (1,)), ((), ())), preferred_element_type=F32)
        scores = scores * (1.0 / math.sqrt(HD))
        place = lax.broadcasted_iota(jnp.int32, scores.shape, 1).astype(F32)
        late = (lax.broadcasted_iota(jnp.int32, scores.shape, 0) >= heads).astype(F32)
        scores = jnp.where(place <= first + late, scores, -jnp.inf)
        probs = jnp.exp(scores - jnp.max(scores, axis=-1, keepdims=True))
        probs = (probs / jnp.sum(probs, axis=-1, keepdims=True)).astype(BF16)
        mixed = jnp.dot(probs, values, preferred_element_type=F32)
        result = mixed[:, :HD]
        for h in range(1, kvs):
            result = jnp.where(kv_q == h, mixed[:, h * HD : (h + 1) * HD], result)
        return result

    @pl.loop(0, req)
    def _(s):
        first = jnp.full((1, 1), tab[at_len + s], jnp.int32).astype(F32)
        fresh = (
            [kr_s[pl.ds(turn * req + s, 1), :] for turn in range(2)],
            [v_s[pl.ds(turn * req + s, 1), :] for turn in range(2)],
        )
        for c in range(pmax):
            at = tab[at_page + s * pmax + c]
            for i in range(2):
                view[i, c * page : (c + 1) * page, :] = inserted(pool[i, at], c, first, fresh[i])
        cosines = [cos_ref[pl.ds(turn * req + s, 1), :] for turn in range(2)]
        sines = [sin_ref[pl.ds(turn * req + s, 1), :] for turn in range(2)]
        m1[pl.ds(s, 2 * heads, stride=req), :] = attend(0, s, cosines, sines, first, view[0], view[1])

    def sums(phase, k):
        return pltpu.make_async_remote_copy(
            src_ref=rs_out.at[phase, k], dst_ref=rs_in.at[phase, k],
            send_sem=rs_ss.at[phase, k], recv_sem=rs_rs.at[phase, k],
            device_id=(me, lax.rem(tp + k, t)), device_id_type=MESH,
        )

    def project(phase):
        for turn in range(2):
            m = jnp.concatenate(
                [m1[(turn * heads + h) * req : (turn * heads + h + 1) * req, :] for h in range(heads)], axis=1
            )
            mix[turn * req : (turn + 1) * req, :] = m
        lhs = mix[...].astype(BF16)

        @pl.loop(1, t + 1)
        def _(kk):
            k = lax.rem(kk, t)
            target = lax.rem(tp + k, t)

            for c in range(width // tile):
                cols = pl.ds(pl.multiple_of(target * width + c * tile, tile), tile)
                rs_out[phase, k, :, c * tile : (c + 1) * tile] = jnp.dot(
                    lhs, wo_b[:, cols], preferred_element_type=F32
                )

            @pl.when(k > 0)
            def _():
                sums(phase, k).start()

    def finish(phase):
        @pl.loop(1, t)
        def _(k):
            sums(phase, k).wait_recv()

        total = rs_out[phase, 0]
        for k in range(1, t):
            total = total + rs_in[phase, k]
        layer[phase * 2 * req : (phase + 1) * 2 * req, :] = total.astype(BF16)

    load_out.wait()
    project(0)

    def put(k):
        return pltpu.make_async_copy(recv.at[k], staged.at[k], out_sem.at[k])

    @pl.loop(0, n)
    def _(k):
        @pl.when(k > 0)
        def _():
            move_ext(k).wait_recv()
            move(k).wait_recv()

        slot = tab[at_slot + k]
        first = ext_in[k, 8:9, 0:1]
        cosines = [ext_in[k, 4 + turn : 5 + turn, :HD] for turn in range(2)]
        sines = [ext_in[k, 6 + turn : 7 + turn, :HD] for turn in range(2)]
        late = lax.broadcasted_iota(jnp.int32, (2 * kvs, HD), 0) >= kvs
        keys = k_s[pl.ds(2 * kvs * req + slot, 2 * kvs, stride=req), :]
        keys = rounded(rotate(keys, jnp.where(late, cosines[1], cosines[0]), jnp.where(late, sines[1], sines[0])))
        fresh = (
            [ext_in[k, turn : turn + 1, :] for turn in range(2)]
            + [
                jnp.concatenate([keys[turn * kvs + h : turn * kvs + h + 1, :] for h in range(kvs)], axis=1)
                for turn in range(2)
            ],
            [ext_in[k, 2 + turn : 3 + turn, :] for turn in range(2)]
            + [v_s[pl.ds((2 + turn) * req + slot, 1), :] for turn in range(2)],
        )
        for c in range(pmax):
            rows = slice(c * page, (c + 1) * page)
            for i in range(2):
                recv[k, i, rows, :] = inserted(recv[k, i, rows, :], c, first, fresh[i])
        put(k).start()
        m2[pl.ds(k, 2 * heads, stride=n), :] = attend(
            2, slot, cosines, sines, first + 2.0, recv[k, 0], recv[k, 1]
        )

    for s in range(req):
        m1[pl.ds(s, 2 * heads, stride=req), :] = m2[pl.ds(tab[at_rel + s], 2 * heads, stride=n), :]
    project(1)
    finish(0)
    finish(1)

    @pl.loop(0, n)
    def _(k):
        put(k).wait()

        @pl.when(k > 0)
        def _():
            move(k).wait_send()
            move_ext(k).wait_send()

    @pl.loop(1, t)
    def _(k):
        sums(0, k).wait_send()
        sums(1, k).wait_send()


def place(req, rel, staged, keys, values, sem):
    copies = []
    for s in range(req):
        for i, dst in enumerate((keys, values)):
            copies.append(pltpu.make_async_copy(staged.at[rel[s], i], dst.at[0, s], sem.at[i, s]))
    for c in copies:
        c.start()
    for c in copies:
        c.wait()


def local(
    x_steps, w_query, w_key, w_value, w_out, k_pool, v_pool, page_table, lengths,
    source_instance, source_slot,
):
    n = lax.axis_size("inst")
    t = lax.axis_size("tp")
    me = lax.axis_index("inst")
    turns, _, req, depth = x_steps.shape
    pages, page, feats = k_pool.shape[1:]
    context = pages // req * page
    heads = w_query.shape[1] // HD
    kvs = feats // HD
    width = w_out.shape[1] // t
    own_len = lengths[0]

    peers = jnp.arange(n, dtype=jnp.int32)
    slots = jnp.arange(req, dtype=jnp.int32)
    incoming = lax.dynamic_index_in_dim(source_instance, me, 0, keepdims=False)
    goes_to = lax.rem(peers + me, n)
    comes_from = lax.rem(me - peers + n, n)
    hit = (peers[None, :, None] == goes_to[:, None, None]) & (source_instance == me)[None]
    own = jnp.sum(jnp.where(hit, source_slot[None], 0), axis=(1, 2))
    taken = jnp.sum(jnp.where(incoming[None, :] == comes_from[:, None], slots[None, :], 0), axis=1)
    rel = lax.rem(me - incoming + n, n)
    table = jnp.concatenate([own, taken, rel, own_len, page_table[0]]).astype(jnp.int32)
    positions = own_len[None, :] + jnp.arange(turns, dtype=jnp.int32)[:, None]
    cosine, sine = angles_of(positions.reshape(-1))
    x = x_steps.reshape(turns * req, depth)

    chunk, tile, bufs = 512, 512, 3
    smem = pl.BlockSpec(memory_space=pltpu.SMEM)
    vmem = pl.BlockSpec(memory_space=pltpu.VMEM)
    hbm = pl.BlockSpec(memory_space=pl.ANY)
    dma = pltpu.SemaphoreType.DMA
    layer, staged = pl.pallas_call(
        functools.partial(fused, n, t, req, page, chunk, tile),
        out_shape=(
            jax.ShapeDtypeStruct((turns * req, width), BF16),
            jax.ShapeDtypeStruct((n, 2, context, feats), BF16),
        ),
        in_specs=[smem, vmem, vmem, vmem] + [hbm] * 6,
        out_specs=(vmem, hbm),
        scratch_shapes=[
            pltpu.VMEM((2, pages, page, feats), BF16),
            pltpu.VMEM((n, 2, context, feats), BF16),
            pltpu.VMEM((n, 2, context, feats), BF16),
            pltpu.VMEM((n, 16, feats), F32),
            pltpu.VMEM((n, 16, feats), F32),
            pltpu.VMEM((2, context, feats), BF16),
            pltpu.VMEM((bufs, chunk, heads * HD), BF16),
            pltpu.VMEM((bufs, chunk, feats), BF16),
            pltpu.VMEM((bufs, chunk, feats), BF16),
            pltpu.VMEM(w_out.shape, BF16),
            pltpu.VMEM((turns * req, heads * HD + 2 * feats), F32),
            pltpu.VMEM((turns * heads * req, HD), F32),
            pltpu.VMEM((turns * kvs * req, HD), F32),
            pltpu.VMEM((2 * req, feats), F32),
            pltpu.VMEM((turns * req, feats), F32),
            pltpu.VMEM((2 * heads * req, HD), F32),
            pltpu.VMEM((2 * heads * n, HD), F32),
            pltpu.VMEM((2 * req, heads * HD), F32),
            pltpu.VMEM((2, t, 2 * req, width), F32),
            pltpu.VMEM((2, t, 2 * req, width), F32),
            dma((2,)), dma((3, bufs)), dma,
            dma((n,)), dma((n,)), dma((n,)), dma((n,)),
            dma((2, t)), dma((2, t)), dma((n,)),
        ],
        compiler_params=pltpu.CompilerParams(
            collective_id=0, has_side_effects=True, vmem_limit_bytes=56 * 1024 * 1024
        ),
        name="decode",
    )(
        table, cosine, sine, x, w_query, w_key, w_value, w_out,
        k_pool.reshape(pages, page, feats), v_pool.reshape(pages, page, feats),
    )
    key_cache, value_cache = pl.pallas_call(
        functools.partial(place, req),
        out_shape=(jax.ShapeDtypeStruct((1, req, context, feats), BF16),) * 2,
        in_specs=[smem, hbm],
        out_specs=(hbm, hbm),
        scratch_shapes=[dma((2, req))],
        name="place",
    )(rel, staged)
    return layer.reshape(turns, 1, req, width), key_cache, value_cache


def solution(mesh):
    in_specs = (
        P(None, "inst", None, None),
        P(None, "tp"),
        P(None, "tp"),
        P(None, "tp"),
        P("tp", None),
        P("inst", None, None, "tp"),
        P("inst", None, None, "tp"),
        P("inst", None),
        P("inst", None),
        P(),
        P(),
    )
    out_specs = (
        P(None, "inst", None, "tp"),
        P("inst", None, None, "tp"),
        P("inst", None, None, "tp"),
    )
    return jax.shard_map(local, mesh=mesh, in_specs=in_specs, out_specs=out_specs, check_vma=False)
```

```python
import functools
import math

import jax
import jax.numpy as jnp
from jax import lax
from jax.experimental import pallas as pl
from jax.experimental.pallas import tpu as pltpu
from jax.sharding import PartitionSpec as P

HD = 128
GROUP = 4
MESH = pl.DeviceIdType.MESH

rope_base = 500000.0
F32 = jnp.float32
BF16 = jnp.bfloat16


def rotate(vectors, cosine, sine):
    return vectors * cosine + pltpu.roll(vectors, HD // 2, 1) * sine


def rounded(value):
    return value.astype(BF16).astype(F32)


def fused(
    n, t, req, page, chunk, tile,
    sources, source_slots, table, lens, x_ref, wq, wk, wv, wo, kp, vp,
    layer, recv,
    pool, send, ext, ext_in, view, wq_b, wk_b, wv_b, wo_b, acc,
    cos_ref, sin_ref, q_s, k_s, kr_s, v_s, m1, m2, mix, rs_out, rs_in, tot,
    pool_sem, w_sem, wo_sem, kv_ss, kv_rs, ex_ss, ex_rs, rs_ss, rs_rs,
):
    me = lax.axis_index("inst")
    tp = lax.axis_index("tp")
    feats = kp.shape[2]
    heads = wq.shape[1] // HD
    kvs = feats // HD
    pmax = kp.shape[0] // req
    depth = wq.shape[0]
    steps = depth // chunk
    bufs = wq_b.shape[0]
    width = layer.shape[1]
    half = n // 2

    def own_slot(k):
        target = lax.rem(me + k, n)
        found = jnp.int32(0)
        for s in range(req):
            found = jnp.where(sources[target, s] == me, source_slots[target, s], found)
        return found

    def taken_slot(k):
        origin = lax.rem(me - k + n, n)
        found = jnp.int32(0)
        for s in range(req):
            found = jnp.where(sources[me, s] == origin, s, found)
        return found

    pools = [pltpu.make_async_copy(src, pool.at[i], pool_sem.at[i]) for i, src in enumerate((kp, vp))]
    for c in pools:
        c.start()

    def weights(i):
        slot = lax.rem(i, bufs)
        rows = pl.ds(pl.multiple_of(i * chunk, chunk), chunk)
        return [
            pltpu.make_async_copy(src.at[rows], dst.at[slot], w_sem.at[j, slot])
            for j, (src, dst) in enumerate(((wq, wq_b), (wk, wk_b), (wv, wv_b)))
        ]

    barrier = pltpu.get_barrier_semaphore()

    @pl.loop(1, n)
    def _(k):
        pl.semaphore_signal(
            barrier, inc=1, device_id=(lax.rem(me + k, n), tp), device_id_type=MESH
        )

    @pl.loop(1, t)
    def _(k):
        pl.semaphore_signal(
            barrier, inc=1, device_id=(me, lax.rem(tp + k, t)), device_id_type=MESH
        )

    for c in pools:
        c.wait()
    for i in range(bufs - 1):
        for c in weights(i):
            c.start()
    pl.semaphore_wait(barrier, n - 1 + t - 1)

    def move(k):
        return pltpu.make_async_remote_copy(
            src_ref=send.at[k], dst_ref=recv.at[k], send_sem=kv_ss.at[k], recv_sem=kv_rs.at[k],
            device_id=(lax.rem(me + k, n), tp), device_id_type=MESH,
        )

    def move_ext(k):
        return pltpu.make_async_remote_copy(
            src_ref=ext.at[k], dst_ref=ext_in.at[k], send_sem=ex_ss.at[k], recv_sem=ex_rs.at[k],
            device_id=(lax.rem(me + k, n), tp), device_id_type=MESH,
        )

    @pl.loop(1, n)
    def _(k):
        slot = own_slot(k)
        for c in range(pmax):
            at = table[0, slot * pmax + c]
            for i in range(2):
                send[k, i, c * page : (c + 1) * page, :] = pool[i, at]
        move(k).start()

    own = own_slot(0)
    for c in range(pmax):
        at = table[0, own * pmax + c]
        for i in range(2):
            recv[0, i, c * page : (c + 1) * page, :] = pool[i, at]

    row_r = lax.broadcasted_iota(jnp.int32, (4 * req, HD), 0)
    spot = row_r // req
    for s in range(req):
        spot = jnp.where(lax.rem(row_r, req) == s, spot + lens[0, s], spot)
    lane = lax.rem(lax.broadcasted_iota(jnp.int32, (4 * req, HD), 1), HD // 2)
    angle = spot.astype(F32) * jnp.exp(lane.astype(F32) * (-2.0 * math.log(rope_base) / HD))
    cos_ref[...] = jnp.cos(angle)
    sine = jnp.sin(angle)
    sin_ref[...] = jnp.where(lax.broadcasted_iota(jnp.int32, sine.shape, 1) < HD // 2, -sine, sine)

    acc[...] = jnp.zeros_like(acc)
    qw = heads * HD

    @pl.loop(0, steps)
    def _(i):
        @pl.when(i + bufs - 1 < steps)
        def _():
            for c in weights(i + bufs - 1):
                c.start()

        for c in weights(i):
            c.wait()
        slot = lax.rem(i, bufs)
        xs = x_ref[:, pl.ds(pl.multiple_of(i * chunk, chunk), chunk)]
        acc[:, :qw] += jnp.dot(xs, wq_b[slot], preferred_element_type=F32)
        acc[:, qw : qw + feats] += jnp.dot(xs, wk_b[slot], preferred_element_type=F32)
        acc[:, qw + feats :] += jnp.dot(xs, wv_b[slot], preferred_element_type=F32)

    load_out = pltpu.make_async_copy(wo, wo_b, wo_sem)
    load_out.start()

    for turn in range(4):
        rows = slice(turn * req, (turn + 1) * req)
        for h in range(heads):
            q_s[(turn * heads + h) * req : (turn * heads + h + 1) * req, :] = acc[rows, h * HD : (h + 1) * HD]
        for h in range(kvs):
            part = acc[rows, qw + h * HD : qw + (h + 1) * HD]
            k_s[(turn * kvs + h) * req : (turn * kvs + h + 1) * req, :] = part
            if turn < 2:
                kr_s[rows, h * HD : (h + 1) * HD] = rounded(rotate(part, cos_ref[rows, :], sin_ref[rows, :]))
    v_s[...] = rounded(acc[:, qw + feats :])

    @pl.loop(0, n)
    def _(k):
        slot = own_slot(k)
        for turn in range(2):
            ext[k, turn : turn + 1, :] = kr_s[pl.ds(turn * req + slot, 1), :]
            ext[k, 2 + turn : 3 + turn, :] = v_s[pl.ds(turn * req + slot, 1), :]
            ext[k, 4 + turn : 5 + turn, :HD] = cos_ref[pl.ds((2 + turn) * req + slot, 1), :]
            ext[k, 6 + turn : 7 + turn, :HD] = sin_ref[pl.ds((2 + turn) * req + slot, 1), :]
        ext[k, 8:9, :] = jnp.full((1, feats), lens[0, slot], jnp.int32).astype(F32)
        ext[k, 9:16, :] = jnp.zeros((7, feats), F32)

        @pl.when(k > 0)
        def _():
            move_ext(k).start()

    ext_in[0] = ext[0]

    spots = lax.broadcasted_iota(jnp.int32, (page, feats), 0).astype(F32)

    def inserted(block, c, first, fresh):
        block = block.astype(F32)
        for i, row in enumerate(fresh):
            block = jnp.where(spots == first + (i - c * page), row, block)
        return block.astype(BF16)

    row_q = lax.broadcasted_iota(jnp.int32, (2 * heads, HD), 0)
    late_q = row_q >= heads
    kv_q = lax.rem(row_q, heads) // GROUP

    def attend(base, slot, cosines, sines, first, keys, values):
        q = q_s[pl.ds(base * heads * req + slot, 2 * heads, stride=req), :]
        cosine = jnp.where(late_q, cosines[1], cosines[0])
        sine = jnp.where(late_q, sines[1], sines[0])
        q = rotate(q, cosine, sine)
        q = jnp.concatenate([jnp.where(kv_q == h, q, 0.0) for h in range(kvs)], axis=1).astype(BF16)
        scores = lax.dot_general(q, keys, (((1,), (1,)), ((), ())), preferred_element_type=F32)
        scores = scores * (1.0 / math.sqrt(HD))
        place = lax.broadcasted_iota(jnp.int32, scores.shape, 1).astype(F32)
        late = (lax.broadcasted_iota(jnp.int32, scores.shape, 0) >= heads).astype(F32)
        scores = jnp.where(place <= first + late, scores, -jnp.inf)
        probs = jnp.exp(scores - jnp.max(scores, axis=-1, keepdims=True))
        probs = (probs / jnp.sum(probs, axis=-1, keepdims=True)).astype(BF16)
        mixed = jnp.dot(probs, values, preferred_element_type=F32)
        result = mixed[:, :HD]
        for h in range(1, kvs):
            result = jnp.where(kv_q == h, mixed[:, h * HD : (h + 1) * HD], result)
        return result

    @pl.loop(0, req)
    def _(s):
        first = jnp.full((1, 1), lens[0, s], jnp.int32).astype(F32)
        fresh = (
            [kr_s[pl.ds(turn * req + s, 1), :] for turn in range(2)],
            [v_s[pl.ds(turn * req + s, 1), :] for turn in range(2)],
        )
        for c in range(pmax):
            at = table[0, s * pmax + c]
            for i in range(2):
                view[i, c * page : (c + 1) * page, :] = inserted(pool[i, at], c, first, fresh[i])
        cosines = [cos_ref[pl.ds(turn * req + s, 1), :] for turn in range(2)]
        sines = [sin_ref[pl.ds(turn * req + s, 1), :] for turn in range(2)]
        m1[pl.ds(s, 2 * heads, stride=req), :] = attend(0, s, cosines, sines, first, view[0], view[1])

    def sums(phase, k):
        return pltpu.make_async_remote_copy(
            src_ref=rs_out.at[phase, k, : 2 * req if phase == 0 else n],
            dst_ref=rs_in.at[phase, k, : 2 * req if phase == 0 else n],
            send_sem=rs_ss.at[phase, k], recv_sem=rs_rs.at[phase, k],
            device_id=(me, lax.rem(tp + k, t)), device_id_type=MESH,
        )

    def project(phase):
        rows = 2 * req if phase == 0 else n
        lhs = mix[:rows, :].astype(BF16)

        @pl.loop(1, t + 1)
        def _(kk):
            k = lax.rem(kk, t)
            target = lax.rem(tp + k, t)

            for c in range(width // tile):
                cols = pl.ds(pl.multiple_of(target * width + c * tile, tile), tile)
                rs_out[phase, k, :rows, c * tile : (c + 1) * tile] = jnp.dot(
                    lhs, wo_b[:, cols], preferred_element_type=F32
                )

            @pl.when(k > 0)
            def _():
                sums(phase, k).start()

    def total_of(phase):
        rows = 2 * req if phase == 0 else n

        @pl.loop(1, t)
        def _(k):
            sums(phase, k).wait_recv()

        total = rs_out[phase, 0, :rows, :]
        for k in range(1, t):
            total = total + rs_in[phase, k, :rows, :]
        return total

    load_out.wait()
    for turn in range(2):
        for h in range(heads):
            at = (turn * heads + h) * req
            mix[turn * req : (turn + 1) * req, h * HD : (h + 1) * HD] = m1[at : at + req, :]
    project(0)

    def arrival(k):
        @pl.when(k > 0)
        def _():
            move_ext(k).wait_recv()
            move(k).wait_recv()

        slot = taken_slot(k)
        first = ext_in[k, 8:9, 0:1]
        cosines = [ext_in[k, 4 + turn : 5 + turn, :HD] for turn in range(2)]
        sines = [ext_in[k, 6 + turn : 7 + turn, :HD] for turn in range(2)]
        late = lax.broadcasted_iota(jnp.int32, (2 * kvs, HD), 0) >= kvs
        keys = k_s[pl.ds(2 * kvs * req + slot, 2 * kvs, stride=req), :]
        keys = rounded(rotate(keys, jnp.where(late, cosines[1], cosines[0]), jnp.where(late, sines[1], sines[0])))
        fresh = (
            [ext_in[k, turn : turn + 1, :] for turn in range(2)]
            + [
                jnp.concatenate([keys[turn * kvs + h : turn * kvs + h + 1, :] for h in range(kvs)], axis=1)
                for turn in range(2)
            ],
            [ext_in[k, 2 + turn : 3 + turn, :] for turn in range(2)]
            + [v_s[pl.ds((2 + turn) * req + slot, 1), :] for turn in range(2)],
        )
        for c in range(pmax):
            rows = slice(c * page, (c + 1) * page)
            for i in range(2):
                recv[k, i, rows, :] = inserted(recv[k, i, rows, :], c, first, fresh[i])
        m2[pl.ds(k, 2 * heads, stride=n), :] = attend(
            2, slot, cosines, sines, first + 2.0, recv[k, 0], recv[k, 1]
        )

    def gathered(group):
        for turn in range(2):
            for h in range(heads):
                at = (turn * heads + h) * n + group * half
                mix[turn * half : (turn + 1) * half, h * HD : (h + 1) * HD] = m2[at : at + half, :]
        project(1 + group)

    pl.loop(0, half)(arrival)
    gathered(0)
    layer[: 2 * req, :] = total_of(0).astype(BF16)
    pl.loop(half, n)(arrival)
    gathered(1)
    for group in range(2):
        tot[group * n : (group + 1) * n, :] = total_of(1 + group)
    rows = []
    for turn in range(2):
        for s in range(req):
            k = lax.rem(me - sources[me, s] + n, n)
            rows.append(tot[pl.ds(k // half * n + turn * half + lax.rem(k, half), 1), :])
    layer[2 * req :, :] = jnp.concatenate(rows, axis=0).astype(BF16)

    @pl.loop(1, n)
    def _(k):
        move(k).wait_send()
        move_ext(k).wait_send()

    @pl.loop(1, t)
    def _(k):
        for phase in range(3):
            sums(phase, k).wait_send()


def place(n, req, sources, staged, keys, values, sem):
    me = lax.axis_index("inst")
    copies = []
    for s in range(req):
        k = lax.rem(me - sources[me, s] + n, n)
        for i, dst in enumerate((keys, values)):
            copies.append(pltpu.make_async_copy(staged.at[k, i], dst.at[0, s], sem.at[i, s]))
            copies[-1].start()
    for c in copies:
        c.wait()


def local(
    x_steps, w_query, w_key, w_value, w_out, k_pool, v_pool, page_table, lengths,
    source_instance, source_slot,
):
    n = lax.axis_size("inst")
    t = lax.axis_size("tp")
    turns, _, req, depth = x_steps.shape
    pages, page, feats = k_pool.shape[1:]
    context = pages // req * page
    heads = w_query.shape[1] // HD
    kvs = feats // HD
    width = w_out.shape[1] // t
    x = x_steps.reshape(turns * req, depth)

    chunk, tile, bufs = 512, 512, 3
    smem = pl.BlockSpec(memory_space=pltpu.SMEM)
    vmem = pl.BlockSpec(memory_space=pltpu.VMEM)
    hbm = pl.BlockSpec(memory_space=pl.ANY)
    dma = pltpu.SemaphoreType.DMA
    layer, staged = pl.pallas_call(
        functools.partial(fused, n, t, req, page, chunk, tile),
        out_shape=(
            jax.ShapeDtypeStruct((turns * req, width), BF16),
            pltpu.VMEM((n, 2, context, feats), BF16),
        ),
        in_specs=[smem] * 4 + [vmem] + [hbm] * 6,
        out_specs=(vmem, vmem),
        scratch_shapes=[
            pltpu.VMEM((2, pages, page, feats), BF16),
            pltpu.VMEM((n, 2, context, feats), BF16),
            pltpu.VMEM((n, 16, feats), F32),
            pltpu.VMEM((n, 16, feats), F32),
            pltpu.VMEM((2, context, feats), BF16),
            pltpu.VMEM((bufs, chunk, heads * HD), BF16),
            pltpu.VMEM((bufs, chunk, feats), BF16),
            pltpu.VMEM((bufs, chunk, feats), BF16),
            pltpu.VMEM(w_out.shape, BF16),
            pltpu.VMEM((turns * req, heads * HD + 2 * feats), F32),
            pltpu.VMEM((turns * req, HD), F32),
            pltpu.VMEM((turns * req, HD), F32),
            pltpu.VMEM((turns * heads * req, HD), F32),
            pltpu.VMEM((turns * kvs * req, HD), F32),
            pltpu.VMEM((2 * req, feats), F32),
            pltpu.VMEM((turns * req, feats), F32),
            pltpu.VMEM((2 * heads * req, HD), F32),
            pltpu.VMEM((2 * heads * n, HD), F32),
            pltpu.VMEM((2 * req, heads * HD), F32),
            pltpu.VMEM((3, t, max(n, 2 * req), width), F32),
            pltpu.VMEM((3, t, max(n, 2 * req), width), F32),
            pltpu.VMEM((2 * n, width), F32),
            dma((2,)), dma((3, bufs)), dma,
            dma((n,)), dma((n,)), dma((n,)), dma((n,)),
            dma((3, t)), dma((3, t)),
        ],
        compiler_params=pltpu.CompilerParams(
            collective_id=0, has_side_effects=True, vmem_limit_bytes=56 * 1024 * 1024
        ),
        name="decode",
    )(
        source_instance, source_slot, page_table, lengths, x, w_query, w_key, w_value, w_out,
        k_pool.reshape(pages, page, feats), v_pool.reshape(pages, page, feats),
    )
    key_cache, value_cache = pl.pallas_call(
        functools.partial(place, n, req),
        out_shape=(jax.ShapeDtypeStruct((1, req, context, feats), BF16),) * 2,
        in_specs=[smem, hbm],
        out_specs=(hbm, hbm),
        scratch_shapes=[dma((2, req))],
        compiler_params=pltpu.CompilerParams(vmem_limit_bytes=56 * 1024 * 1024),
        name="place",
    )(source_instance, pltpu.with_memory_space_constraint(staged, pltpu.VMEM))
    return layer.reshape(turns, 1, req, width), key_cache, value_cache


def solution(mesh):
    in_specs = (
        P(None, "inst", None, None),
        P(None, "tp"),
        P(None, "tp"),
        P(None, "tp"),
        P("tp", None),
        P("inst", None, None, "tp"),
        P("inst", None, None, "tp"),
        P("inst", None),
        P("inst", None),
        P(),
        P(),
    )
    out_specs = (
        P(None, "inst", None, "tp"),
        P("inst", None, None, "tp"),
        P("inst", None, None, "tp"),
    )
    return jax.shard_map(local, mesh=mesh, in_specs=in_specs, out_specs=out_specs, check_vma=False)
```

```python
import functools
import math

import jax
import jax.numpy as jnp
from jax import lax
from jax.experimental import pallas as pl
from jax.experimental.pallas import tpu as pltpu
from jax.sharding import PartitionSpec as P

HD = 128
GROUP = 4
MESH = pl.DeviceIdType.MESH

rope_base = 500000.0
F32 = jnp.float32
BF16 = jnp.bfloat16


def offset_of(k, n):
    return lax.rem(2 * k, n) + k // (n // 2)


def move_of(offset, n):
    return offset // 2 + lax.rem(offset, 2) * (n // 2)


def rotate(vectors, cosine, sine):
    return vectors * cosine + pltpu.roll(vectors, HD // 2, 1) * sine


def rounded(value):
    return value.astype(BF16).astype(F32)


def fused(
    n, t, req, page, chunk, tile,
    sources, source_slots, table, lens, x_ref, wq, wk, wv, wo, kp, vp,
    layer, recv,
    pool, send, ext, ext_in, view, wq_b, wk_b, wv_b, wo_b, acc,
    cos_ref, sin_ref, q_s, k_s, kr_s, v_s, m1, m2, mix, rs_out, rs_in, tot,
    pool_sem, w_sem, wo_sem, kv_ss, kv_rs, ex_ss, ex_rs, rs_ss, rs_rs,
):
    me = lax.axis_index("inst")
    tp = lax.axis_index("tp")
    feats = kp.shape[2]
    heads = wq.shape[1] // HD
    kvs = feats // HD
    pmax = kp.shape[0] // req
    depth = wq.shape[0]
    steps = depth // chunk
    bufs = wq_b.shape[0]
    width = layer.shape[1]
    half = n // 2

    def own_slot(k):
        target = lax.rem(me + offset_of(k, n), n)
        found = jnp.int32(0)
        for s in range(req):
            found = jnp.where(sources[target, s] == me, source_slots[target, s], found)
        return found

    def taken_slot(k):
        origin = lax.rem(me - offset_of(k, n) + n, n)
        found = jnp.int32(0)
        for s in range(req):
            found = jnp.where(sources[me, s] == origin, s, found)
        return found

    pools = [pltpu.make_async_copy(src, pool.at[i], pool_sem.at[i]) for i, src in enumerate((kp, vp))]
    for c in pools:
        c.start()

    def weights(i):
        slot = lax.rem(i, bufs)
        rows = pl.ds(pl.multiple_of(i * chunk, chunk), chunk)
        return [
            pltpu.make_async_copy(src.at[rows], dst.at[slot], w_sem.at[j, slot])
            for j, (src, dst) in enumerate(((wq, wq_b), (wk, wk_b), (wv, wv_b)))
        ]

    barrier = pltpu.get_barrier_semaphore()

    @pl.loop(1, n)
    def _(k):
        pl.semaphore_signal(
            barrier, inc=1, device_id=(lax.rem(me + k, n), tp), device_id_type=MESH
        )

    @pl.loop(1, t)
    def _(k):
        pl.semaphore_signal(
            barrier, inc=1, device_id=(me, lax.rem(tp + k, t)), device_id_type=MESH
        )

    for c in pools:
        c.wait()
    for i in range(bufs - 1):
        for c in weights(i):
            c.start()
    pl.semaphore_wait(barrier, n - 1 + t - 1)

    def move(k):
        return pltpu.make_async_remote_copy(
            src_ref=send.at[k], dst_ref=recv.at[k], send_sem=kv_ss.at[k], recv_sem=kv_rs.at[k],
            device_id=(lax.rem(me + offset_of(k, n), n), tp), device_id_type=MESH,
        )

    def move_ext(k):
        return pltpu.make_async_remote_copy(
            src_ref=ext.at[k], dst_ref=ext_in.at[k], send_sem=ex_ss.at[k], recv_sem=ex_rs.at[k],
            device_id=(lax.rem(me + offset_of(k, n), n), tp), device_id_type=MESH,
        )

    def depart(k):
        slot = own_slot(k)
        for c in range(pmax):
            at = table[0, slot * pmax + c]
            for i in range(2):
                send[k, i, c * page : (c + 1) * page, :] = pool[i, at]
        move(k).start()

    pl.loop(1, half)(depart)
    own = own_slot(0)
    for c in range(pmax):
        at = table[0, own * pmax + c]
        for i in range(2):
            recv[0, i, c * page : (c + 1) * page, :] = pool[i, at]

    row_r = lax.broadcasted_iota(jnp.int32, (4 * req, HD), 0)
    spot = row_r // req
    for s in range(req):
        spot = jnp.where(lax.rem(row_r, req) == s, spot + lens[0, s], spot)
    lane = lax.rem(lax.broadcasted_iota(jnp.int32, (4 * req, HD), 1), HD // 2)
    angle = spot.astype(F32) * jnp.exp(lane.astype(F32) * (-2.0 * math.log(rope_base) / HD))
    cos_ref[...] = jnp.cos(angle)
    sine = jnp.sin(angle)
    sin_ref[...] = jnp.where(lax.broadcasted_iota(jnp.int32, sine.shape, 1) < HD // 2, -sine, sine)

    acc[...] = jnp.zeros_like(acc)
    qw = heads * HD

    @pl.loop(0, steps)
    def _(i):
        @pl.when(i + bufs - 1 < steps)
        def _():
            for c in weights(i + bufs - 1):
                c.start()

        for c in weights(i):
            c.wait()
        slot = lax.rem(i, bufs)
        xs = x_ref[:, pl.ds(pl.multiple_of(i * chunk, chunk), chunk)]
        acc[:, :qw] += jnp.dot(xs, wq_b[slot], preferred_element_type=F32)
        acc[:, qw : qw + feats] += jnp.dot(xs, wk_b[slot], preferred_element_type=F32)
        acc[:, qw + feats :] += jnp.dot(xs, wv_b[slot], preferred_element_type=F32)

    load_out = pltpu.make_async_copy(wo, wo_b, wo_sem)
    load_out.start()

    for turn in range(4):
        rows = slice(turn * req, (turn + 1) * req)
        for h in range(heads):
            q_s[(turn * heads + h) * req : (turn * heads + h + 1) * req, :] = acc[rows, h * HD : (h + 1) * HD]
        for h in range(kvs):
            part = acc[rows, qw + h * HD : qw + (h + 1) * HD]
            k_s[(turn * kvs + h) * req : (turn * kvs + h + 1) * req, :] = part
            if turn < 2:
                kr_s[rows, h * HD : (h + 1) * HD] = rounded(rotate(part, cos_ref[rows, :], sin_ref[rows, :]))
    v_s[...] = rounded(acc[:, qw + feats :])

    @pl.loop(0, n)
    def _(k):
        slot = own_slot(k)
        for turn in range(2):
            ext[k, turn : turn + 1, :] = kr_s[pl.ds(turn * req + slot, 1), :]
            ext[k, 2 + turn : 3 + turn, :] = v_s[pl.ds(turn * req + slot, 1), :]
            ext[k, 4 + turn : 5 + turn, :HD] = cos_ref[pl.ds((2 + turn) * req + slot, 1), :]
            ext[k, 6 + turn : 7 + turn, :HD] = sin_ref[pl.ds((2 + turn) * req + slot, 1), :]
        ext[k, 8:9, :] = jnp.full((1, feats), lens[0, slot], jnp.int32).astype(F32)
        ext[k, 9:16, :] = jnp.zeros((7, feats), F32)

        @pl.when(k > 0)
        def _():
            move_ext(k).start()

    ext_in[0] = ext[0]

    spots = lax.broadcasted_iota(jnp.int32, (page, feats), 0).astype(F32)

    def inserted(block, c, first, fresh):
        block = block.astype(F32)
        for i, row in enumerate(fresh):
            block = jnp.where(spots == first + (i - c * page), row, block)
        return block.astype(BF16)

    row_q = lax.broadcasted_iota(jnp.int32, (2 * heads, HD), 0)
    late_q = row_q >= heads
    kv_q = lax.rem(row_q, heads) // GROUP

    def attend(base, slot, cosines, sines, first, keys, values):
        q = q_s[pl.ds(base * heads * req + slot, 2 * heads, stride=req), :]
        cosine = jnp.where(late_q, cosines[1], cosines[0])
        sine = jnp.where(late_q, sines[1], sines[0])
        q = rotate(q, cosine, sine)
        q = jnp.concatenate([jnp.where(kv_q == h, q, 0.0) for h in range(kvs)], axis=1).astype(BF16)
        scores = lax.dot_general(q, keys, (((1,), (1,)), ((), ())), preferred_element_type=F32)
        scores = scores * (1.0 / math.sqrt(HD))
        place = lax.broadcasted_iota(jnp.int32, scores.shape, 1).astype(F32)
        late = (lax.broadcasted_iota(jnp.int32, scores.shape, 0) >= heads).astype(F32)
        scores = jnp.where(place <= first + late, scores, -jnp.inf)
        probs = jnp.exp(scores - jnp.max(scores, axis=-1, keepdims=True))
        probs = (probs / jnp.sum(probs, axis=-1, keepdims=True)).astype(BF16)
        mixed = jnp.dot(probs, values, preferred_element_type=F32)
        result = mixed[:, :HD]
        for h in range(1, kvs):
            result = jnp.where(kv_q == h, mixed[:, h * HD : (h + 1) * HD], result)
        return result

    @pl.loop(0, req)
    def _(s):
        first = jnp.full((1, 1), lens[0, s], jnp.int32).astype(F32)
        fresh = (
            [kr_s[pl.ds(turn * req + s, 1), :] for turn in range(2)],
            [v_s[pl.ds(turn * req + s, 1), :] for turn in range(2)],
        )
        for c in range(pmax):
            at = table[0, s * pmax + c]
            for i in range(2):
                view[i, c * page : (c + 1) * page, :] = inserted(pool[i, at], c, first, fresh[i])
        cosines = [cos_ref[pl.ds(turn * req + s, 1), :] for turn in range(2)]
        sines = [sin_ref[pl.ds(turn * req + s, 1), :] for turn in range(2)]
        m1[pl.ds(s, 2 * heads, stride=req), :] = attend(0, s, cosines, sines, first, view[0], view[1])

    pl.loop(half, n)(depart)

    def sums(phase, k):
        return pltpu.make_async_remote_copy(
            src_ref=rs_out.at[phase, k, : 2 * req if phase == 0 else n],
            dst_ref=rs_in.at[phase, k, : 2 * req if phase == 0 else n],
            send_sem=rs_ss.at[phase, k], recv_sem=rs_rs.at[phase, k],
            device_id=(me, lax.rem(tp + k, t)), device_id_type=MESH,
        )

    def project(phase):
        rows = 2 * req if phase == 0 else n
        lhs = mix[:rows, :].astype(BF16)

        @pl.loop(1, t + 1)
        def _(kk):
            k = lax.rem(kk, t)
            target = lax.rem(tp + k, t)

            for c in range(width // tile):
                cols = pl.ds(pl.multiple_of(target * width + c * tile, tile), tile)
                rs_out[phase, k, :rows, c * tile : (c + 1) * tile] = jnp.dot(
                    lhs, wo_b[:, cols], preferred_element_type=F32
                )

            @pl.when(k > 0)
            def _():
                sums(phase, k).start()

    def total_of(phase):
        rows = 2 * req if phase == 0 else n

        @pl.loop(1, t)
        def _(k):
            sums(phase, k).wait_recv()

        total = rs_out[phase, 0, :rows, :]
        for k in range(1, t):
            total = total + rs_in[phase, k, :rows, :]
        return total

    load_out.wait()
    for turn in range(2):
        for h in range(heads):
            at = (turn * heads + h) * req
            mix[turn * req : (turn + 1) * req, h * HD : (h + 1) * HD] = m1[at : at + req, :]
    project(0)

    def arrival(k):
        @pl.when(k > 0)
        def _():
            move_ext(k).wait_recv()
            move(k).wait_recv()

        slot = taken_slot(k)
        first = ext_in[k, 8:9, 0:1]
        cosines = [ext_in[k, 4 + turn : 5 + turn, :HD] for turn in range(2)]
        sines = [ext_in[k, 6 + turn : 7 + turn, :HD] for turn in range(2)]
        late = lax.broadcasted_iota(jnp.int32, (2 * kvs, HD), 0) >= kvs
        keys = k_s[pl.ds(2 * kvs * req + slot, 2 * kvs, stride=req), :]
        keys = rounded(rotate(keys, jnp.where(late, cosines[1], cosines[0]), jnp.where(late, sines[1], sines[0])))
        fresh = (
            [ext_in[k, turn : turn + 1, :] for turn in range(2)]
            + [
                jnp.concatenate([keys[turn * kvs + h : turn * kvs + h + 1, :] for h in range(kvs)], axis=1)
                for turn in range(2)
            ],
            [ext_in[k, 2 + turn : 3 + turn, :] for turn in range(2)]
            + [v_s[pl.ds((2 + turn) * req + slot, 1), :] for turn in range(2)],
        )
        for c in range(pmax):
            rows = slice(c * page, (c + 1) * page)
            for i in range(2):
                recv[k, i, rows, :] = inserted(recv[k, i, rows, :], c, first, fresh[i])
        m2[pl.ds(k, 2 * heads, stride=n), :] = attend(
            2, slot, cosines, sines, first + 2.0, recv[k, 0], recv[k, 1]
        )

    def gathered(group):
        for turn in range(2):
            for h in range(heads):
                at = (turn * heads + h) * n + group * half
                mix[turn * half : (turn + 1) * half, h * HD : (h + 1) * HD] = m2[at : at + half, :]
        project(1 + group)

    pl.loop(0, half)(arrival)
    gathered(0)
    layer[: 2 * req, :] = total_of(0).astype(BF16)
    pl.loop(half, n)(arrival)
    gathered(1)
    for group in range(2):
        tot[group * n : (group + 1) * n, :] = total_of(1 + group)
    rows = []
    for turn in range(2):
        for s in range(req):
            k = move_of(lax.rem(me - sources[me, s] + n, n), n)
            rows.append(tot[pl.ds(k // half * n + turn * half + lax.rem(k, half), 1), :])
    layer[2 * req :, :] = jnp.concatenate(rows, axis=0).astype(BF16)

    @pl.loop(1, n)
    def _(k):
        move(k).wait_send()
        move_ext(k).wait_send()

    @pl.loop(1, t)
    def _(k):
        for phase in range(3):
            sums(phase, k).wait_send()


def place(n, req, sources, staged, keys, values, sem):
    me = lax.axis_index("inst")
    copies = []
    for s in range(req):
        k = move_of(lax.rem(me - sources[me, s] + n, n), n)
        for i, dst in enumerate((keys, values)):
            copies.append(pltpu.make_async_copy(staged.at[k, i], dst.at[0, s], sem.at[i, s]))
            copies[-1].start()
    for c in copies:
        c.wait()


def local(
    x_steps, w_query, w_key, w_value, w_out, k_pool, v_pool, page_table, lengths,
    source_instance, source_slot,
):
    n = lax.axis_size("inst")
    t = lax.axis_size("tp")
    turns, _, req, depth = x_steps.shape
    pages, page, feats = k_pool.shape[1:]
    context = pages // req * page
    heads = w_query.shape[1] // HD
    kvs = feats // HD
    width = w_out.shape[1] // t
    x = x_steps.reshape(turns * req, depth)

    chunk, tile, bufs = 512, 512, 3
    smem = pl.BlockSpec(memory_space=pltpu.SMEM)
    vmem = pl.BlockSpec(memory_space=pltpu.VMEM)
    hbm = pl.BlockSpec(memory_space=pl.ANY)
    dma = pltpu.SemaphoreType.DMA
    layer, staged = pl.pallas_call(
        functools.partial(fused, n, t, req, page, chunk, tile),
        out_shape=(
            jax.ShapeDtypeStruct((turns * req, width), BF16),
            pltpu.VMEM((n, 2, context, feats), BF16),
        ),
        in_specs=[smem] * 4 + [vmem] + [hbm] * 6,
        out_specs=(vmem, vmem),
        scratch_shapes=[
            pltpu.VMEM((2, pages, page, feats), BF16),
            pltpu.VMEM((n, 2, context, feats), BF16),
            pltpu.VMEM((n, 16, feats), F32),
            pltpu.VMEM((n, 16, feats), F32),
            pltpu.VMEM((2, context, feats), BF16),
            pltpu.VMEM((bufs, chunk, heads * HD), BF16),
            pltpu.VMEM((bufs, chunk, feats), BF16),
            pltpu.VMEM((bufs, chunk, feats), BF16),
            pltpu.VMEM(w_out.shape, BF16),
            pltpu.VMEM((turns * req, heads * HD + 2 * feats), F32),
            pltpu.VMEM((turns * req, HD), F32),
            pltpu.VMEM((turns * req, HD), F32),
            pltpu.VMEM((turns * heads * req, HD), F32),
            pltpu.VMEM((turns * kvs * req, HD), F32),
            pltpu.VMEM((2 * req, feats), F32),
            pltpu.VMEM((turns * req, feats), F32),
            pltpu.VMEM((2 * heads * req, HD), F32),
            pltpu.VMEM((2 * heads * n, HD), F32),
            pltpu.VMEM((2 * req, heads * HD), F32),
            pltpu.VMEM((3, t, max(n, 2 * req), width), F32),
            pltpu.VMEM((3, t, max(n, 2 * req), width), F32),
            pltpu.VMEM((2 * n, width), F32),
            dma((2,)), dma((3, bufs)), dma,
            dma((n,)), dma((n,)), dma((n,)), dma((n,)),
            dma((3, t)), dma((3, t)),
        ],
        compiler_params=pltpu.CompilerParams(
            collective_id=0, has_side_effects=True, vmem_limit_bytes=56 * 1024 * 1024
        ),
        name="decode",
    )(
        source_instance, source_slot, page_table, lengths, x, w_query, w_key, w_value, w_out,
        k_pool.reshape(pages, page, feats), v_pool.reshape(pages, page, feats),
    )
    key_cache, value_cache = pl.pallas_call(
        functools.partial(place, n, req),
        out_shape=(jax.ShapeDtypeStruct((1, req, context, feats), BF16),) * 2,
        in_specs=[smem, hbm],
        out_specs=(hbm, hbm),
        scratch_shapes=[dma((2, req))],
        compiler_params=pltpu.CompilerParams(vmem_limit_bytes=56 * 1024 * 1024),
        name="place",
    )(source_instance, pltpu.with_memory_space_constraint(staged, pltpu.VMEM))
    return layer.reshape(turns, 1, req, width), key_cache, value_cache


def solution(mesh):
    in_specs = (
        P(None, "inst", None, None),
        P(None, "tp"),
        P(None, "tp"),
        P(None, "tp"),
        P("tp", None),
        P("inst", None, None, "tp"),
        P("inst", None, None, "tp"),
        P("inst", None),
        P("inst", None),
        P(),
        P(),
    )
    out_specs = (
        P(None, "inst", None, "tp"),
        P("inst", None, None, "tp"),
        P("inst", None, None, "tp"),
    )
    return jax.shard_map(local, mesh=mesh, in_specs=in_specs, out_specs=out_specs, check_vma=False)
```
